1024 devices in a mesh: freq: 64 (over z, core), srow: 4 (over y), rcol: 4 (over x).
Axes of the slice: x: 4, y: 4, z: 32, core: 2. Of those that a mesh axis runs over, the one named last changes fastest.
Arguments:
- data_time: bfloat16 [48, 2, 128, 128, 1024], P(('srow', 'rcol'), None, 'freq'), may hold values from -6 to 6
- block_cols: int32 [48, 2], P(('srow', 'rcol')), may hold values from 0 to 47, as said below
- row_counts: int32 [48], P(('srow', 'rcol')), may hold values from 1 to 2, as said below
Outputs:
- predicted: bfloat16 [64, 2, 48, 2, 128, 128], P('freq', None, ('srow', 'rcol'))
The draws below stay inside these ranges and needn't reach their ends.
Inputs may be any that keep to these rules, and one draw needn't show every extreme that they name: Each block_cols[i, w] lies within 1 of i; the 2 entries of a row differ. Slots w < row_counts[i] of row i are live; the others are ignored.
All inputs are finite; a program needn't handle non-finite values.
Results may differ from the reference program's by a relative error of at most 0.0076.
Values may be sent and summed in bfloat16 or wider, within the bound.
A program may use at most 32 MiB of HBM per device.

```python
import math
import jax
import jax.numpy as jnp
from jax import lax

BS = 128
NT = 1024
SLOTS = 2
NB = 48
NF = 64


def draw_block_cols(key, part):
    key = jax.random.fold_in(key, 11)
    row_index = jnp.arange(NB, dtype=jnp.int32)
    candidates = row_index[:, None] + jnp.arange(3, dtype=jnp.int32)[None, :] - 1
    outside = ((candidates < 0) | (candidates >= NB)).astype(jnp.int32)
    scores = jax.random.randint(key, (NB, 3), 0, 1 << 20) * 4 + jnp.arange(3, dtype=jnp.int32)[None, :] + outside * (1 << 24)
    ordering = jnp.argsort(scores, axis=1)[:, :SLOTS]
    return jnp.take_along_axis(candidates, ordering, axis=1).astype(jnp.int32)


def draw_row_counts(key, part):
    key = jax.random.fold_in(key, 23)
    count_key, pick_key = jax.random.split(key)
    counts = jax.random.randint(count_key, (NB,), 1, SLOTS + 1)
    chosen = jax.random.randint(pick_key, (), 0, NB)
    return jnp.where(jnp.arange(NB) == chosen, SLOTS, counts).astype(jnp.int32)


def levels(rng, extent, cuts, low, top_value):
    factor_of, own = 1.0, jax.random.fold_in(rng, 6)
    for dim, shards_of in cuts:
        heights = jnp.exp(jax.random.uniform(jax.random.fold_in(own, dim), (shards_of,), jnp.float32, low / len(cuts), top_value / len(cuts)))
        factor_of = factor_of * jnp.repeat(heights, extent[dim] // shards_of).reshape([-1 if axis == dim else 1 for axis in range(len(extent))])
    return factor_of


def scatter_about(key, extent, deviation, bound, cuts=(), kind=jnp.bfloat16):
    values = jax.random.normal(key, extent, jnp.float32) * deviation
    if len(cuts) > 0:
        values = levels(key, extent, cuts, -0.22, 0.18) * values
    return jnp.clip(values, min=-bound, max=bound).astype(kind)


def setup_inputs(seed: int = 0) -> dict:
    arg_keys = jax.random.split(jax.random.key(seed), 4)
    data_time = scatter_about(arg_keys[0], (NB, SLOTS, BS, BS, NT), 1.0, 6.0, ((0, 16), (2, 64)))
    block_cols = draw_block_cols(jax.random.fold_in(arg_keys[3], 71), 0)
    row_counts = draw_row_counts(jax.random.fold_in(arg_keys[3], 71), 0)
    return {"data_time": data_time, "block_cols": block_cols, "row_counts": row_counts}


def spectral_table():
    time_index = jnp.arange(NT, dtype=jnp.int32)
    freq_bins = jnp.arange(NF, dtype=jnp.int32) + 1
    phase_int = time_index[:, None] * freq_bins[None, :] % NT
    angles = phase_int.astype(jnp.float32) * (2.0 * math.pi / NT)
    norm_factor = 1.0 / math.sqrt(NT)
    return (jnp.stack([jnp.cos(angles), -jnp.sin(angles)], axis=1) * norm_factor).astype(jnp.bfloat16)

def multiply(left_part, right_part):
    return jnp.einsum('rab,rbd->rad', left_part.astype(jnp.float32), right_part.astype(jnp.float32))

def complex_product(left_band, extended, row_count, scale_factor):
    outputs = []
    for target in range(3):
        left_parts = []
        right_parts = []
        for source in range(3):
            inner_off = target - source + 1
            if 0 <= inner_off <= 2:
                left_parts.append(left_band[:, :, source])
                right_parts.append(extended[:, source:source + row_count, inner_off])
        left_all = jnp.concatenate(left_parts, axis=3)
        right_all = jnp.concatenate(right_parts, axis=2)
        real_part = multiply(left_all[0], right_all[0]) - multiply(left_all[1], right_all[1])
        imag_part = multiply(left_all[0], right_all[1]) + multiply(left_all[1], right_all[0])
        outputs.append(jnp.stack([real_part, imag_part]) * scale_factor)
    return jnp.stack(outputs, axis=2)

def reference(data_time, block_cols, row_counts):
    table = spectral_table().astype(jnp.float32)

    def row_spectrum(row_data):
        return jnp.einsum('wsrt,tcf->fcwsr', row_data.astype(jnp.float32), table).astype(jnp.bfloat16)
    spectrum = lax.map(row_spectrum, data_time)
    spectrum = jnp.moveaxis(spectrum, 0, 2)
    row_index = jnp.arange(NB, dtype=jnp.int32)
    offsets = block_cols - row_index[:, None] + 1
    live_slot = jnp.arange(SLOTS, dtype=jnp.int32)[None, :] < row_counts[:, None]
    select = ((offsets[:, :, None] == jnp.arange(3, dtype=jnp.int32)[None, None, :]) & live_slot[:, :, None]).astype(jnp.float32)
    scale_factor = (3.0 * BS) ** (-0.5)

    def one_frequency(spec_slice):
        band_rows = jnp.einsum('iwo,ciwab->cioab', select, spec_slice.astype(jnp.float32)).astype(jnp.bfloat16)
        padding = ((0, 0), (1, 1), (0, 0), (0, 0), (0, 0))
        first_order = complex_product(band_rows, jnp.pad(band_rows, padding), NB, scale_factor).astype(jnp.bfloat16)
        second_order = complex_product(band_rows, jnp.pad(first_order, padding), NB, scale_factor)
        difference = first_order.astype(jnp.float32) - second_order
        return jnp.einsum('iwo,cioab->ciwab', select, difference).astype(jnp.bfloat16)
    return lax.map(one_frequency, spectrum)
```

```python
import functools
import math

import jax
import jax.numpy as jnp
import numpy as np
from jax import lax
from jax.experimental import pallas as pl
from jax.experimental.pallas import tpu as pltpu
from jax.sharding import PartitionSpec as P

BS = 128
PAIR = 2 * BS
ROWS = 3
SLOTS = 2
GROUP = 8
MESH = pl.DeviceIdType.MESH


def spectral_table(samples, freq_count):
    time_index = np.arange(samples, dtype=np.int64)
    freq_bins = np.arange(freq_count, dtype=np.int64) + 1
    phase_int = freq_bins[:, None] * time_index[None, :] % samples
    angles = phase_int.astype(np.float32) * np.float32(2.0 * math.pi / samples)
    table = np.concatenate([np.cos(angles), -np.sin(angles)], axis=0)
    return (table * np.float32(1.0 / math.sqrt(samples))).astype(jnp.bfloat16)


def kernel(
    freqs, srows, rcols,
    x_hbm, table_hbm, meta_ref, out_ref,
    xv, tv, spread, sendbuf, recv, above, below, meta_up, meta_down, gather, bands, firsts,
    load_sem, table_sem, own_sem, send_sem, recv_sem, fsend_sem, frecv_sem, msend_sem, mrecv_sem,
):
    chips = freqs // 2
    me = lax.axis_index("freq")
    zpos, core = me // 2, me % 2
    grow = lax.axis_index("srow") * rcols + lax.axis_index("rcol")
    groups = srows * rcols
    nxt, prv = (grow + 1) % groups, (grow + groups - 1) % groups
    nxt_id = (me, nxt // rcols, nxt % rcols)
    prv_id = (me, prv // rcols, prv % rcols)
    pairs = ROWS * SLOTS

    table_copy = pltpu.make_async_copy(table_hbm, tv, table_sem)
    table_copy.start()
    loads = [pltpu.make_async_copy(x_hbm.at[n], xv.at[n], load_sem.at[n]) for n in range(pairs)]
    for load in loads:
        load.start()

    barrier = pltpu.get_barrier_semaphore()

    def greet(n, carry):
        pl.semaphore_signal(
            barrier, inc=1, device_id={"freq": (me + n) % freqs}, device_id_type=MESH
        )
        return carry

    lax.fori_loop(1, freqs, greet, 0)
    pl.semaphore_signal(barrier, inc=1, device_id=nxt_id, device_id_type=MESH)
    pl.semaphore_signal(barrier, inc=1, device_id=prv_id, device_id_type=MESH)

    table_copy.wait()
    for n in range(pairs):
        loads[n].wait()
        row, slot = n // SLOTS, n % SLOTS
        value = lax.dot_general(
            tv[...], xv[n], (((1,), (1,)), ((), ())), preferred_element_type=jnp.float32
        )
        for part in range(2):
            for trace in range(2):
                place = row * 8 + part * 4 + slot * 2 + trace
                spread[pl.ds(place, freqs, stride=ROWS * 8), :] = value[
                    part * freqs : (part + 1) * freqs, trace * BS : (trace + 1) * BS
                ]
    sendbuf[...] = spread[...].reshape(freqs, ROWS, 8, BS).astype(jnp.bfloat16)

    pl.semaphore_wait(barrier, freqs + 1)

    own_copy = pltpu.make_async_copy(
        sendbuf.at[me], recv.at[2 * (chips - 1) + core], own_sem
    )
    own_copy.start()

    def chip_of(step, sign):
        reach = chips // 2 - (step + 1) // 2
        way = 1 - 2 * ((step + 1) % 2)
        return (zpos + chips + sign * way * reach) % chips

    def send_to(step, other, target):
        return pltpu.make_async_remote_copy(
            src_ref=sendbuf.at[target],
            dst_ref=recv.at[2 * step + core],
            send_sem=send_sem,
            recv_sem=recv_sem.at[step // (GROUP // 2)],
            device_id={"freq": target},
            device_id_type=MESH,
        )

    def send(step, carry):
        chip = chip_of(step, 1)
        for other in range(2):
            send_to(step, other, 2 * chip + other).start()
        return carry

    lax.fori_loop(0, chips - 1, send, 0)
    send_to(chips - 1, 0, 2 * zpos + (1 - core)).start()

    def remote(src, dst, ssem, rsem, target):
        return pltpu.make_async_remote_copy(
            src_ref=src, dst_ref=dst, send_sem=ssem, recv_sem=rsem,
            device_id=target, device_id_type=MESH,
        )

    meta_copies = [
        remote(meta_ref, meta_up, msend_sem.at[0], mrecv_sem.at[0], nxt_id),
        remote(meta_ref, meta_down, msend_sem.at[1], mrecv_sem.at[1], prv_id),
    ]
    for copy in meta_copies:
        copy.start()

    arrival = lax.broadcasted_iota(jnp.int32, (1, 8 * freqs), 1)
    step = arrival >> 4
    reach = chips // 2 - ((step + 1) >> 1)
    way = 1 - 2 * ((step + 1) & 1)
    origin = ((zpos + chips - way * reach) & (chips - 1)) * 2 + ((arrival >> 3) & 1)
    key_in = origin * 8 + (arrival & 7)
    place = lax.broadcasted_iota(jnp.int32, (8 * freqs, 1), 0)
    trace_index = place & (BS - 1)
    key_out = (
        (trace_index >> 1) * 8
        + ((place >> 7) & 1) * 4
        + ((place >> 8) & 1) * 2
        + (trace_index & 1)
    )
    gather[...] = jnp.where(key_in == key_out, 1.0, 0.0).astype(jnp.bfloat16)

    batches = freqs // GROUP

    def border(first):
        span = pl.ds(first, GROUP)
        return (
            remote(recv.at[span, pl.ds(0, 2)], below.at[span], fsend_sem.at[0], frecv_sem.at[0], prv_id),
            remote(recv.at[span, pl.ds(1, 2)], above.at[span], fsend_sem.at[1], frecv_sem.at[1], nxt_id),
        )

    def relay(batch, carry):
        span = recv.at[pl.ds(batch * GROUP, GROUP)]
        remote(span, span, send_sem, recv_sem.at[batch], prv_id).wait_recv()
        for copy in border(batch * GROUP):
            copy.start()
        return carry

    lax.fori_loop(0, batches - 1, relay, 0)
    span = recv.at[pl.ds(0, GROUP - 1)]
    remote(span, span, send_sem, recv_sem.at[batches - 1], prv_id).wait_recv()
    own_copy.wait()
    for copy in border((batches - 1) * GROUP):
        copy.start()

    def rows_of(ref, index):
        return ref[:, index].astype(jnp.float32).reshape(8 * freqs, BS).astype(jnp.bfloat16)

    def place_band(row, block, offsets):
        for shift in range(3):
            parts = []
            for part in range(2):
                total = None
                for slot in range(SLOTS):
                    first = slot * PAIR + part * BS
                    live = jnp.where(offsets[slot] == float(shift), block[first : first + BS], 0.0)
                    total = live if total is None else total + live
                parts.append(total)
            bands[row, shift, :BS, :BS] = parts[0].astype(jnp.bfloat16)
            bands[row, shift, :BS, BS:] = parts[1].astype(jnp.bfloat16)
            bands[row, shift, BS:, :BS] = (-parts[1]).astype(jnp.bfloat16)
            bands[row, shift, BS:, BS:] = parts[0].astype(jnp.bfloat16)

    def assemble(ref, indices, rows, meta):
        stacked = [rows_of(ref, index) for index in indices]
        joined = stacked[0] if len(stacked) == 1 else jnp.concatenate(stacked, axis=1)
        blocks = jnp.dot(gather[...], joined, preferred_element_type=jnp.float32)
        for n, (index, row) in enumerate(zip(indices, rows)):
            offsets = [meta[2 * index + slot : 2 * index + slot + 1, :] for slot in range(SLOTS)]
            place_band(row, blocks[:, n * BS : (n + 1) * BS], offsets)

    scale = (3.0 * BS) ** (-0.5)

    def product(row, target, right, shift_row):
        total = None
        for source in range(3):
            inner = target - source + 1
            if 0 <= inner <= 2:
                term = jnp.dot(
                    bands[row, source, :BS, :],
                    right[row + source - 1 - shift_row, inner],
                    preferred_element_type=jnp.float32,
                )
                total = term if total is None else total + term
        return total * scale

    def first_row(row):
        for target in range(3):
            value = product(row, target, bands, 0).astype(jnp.bfloat16)
            firsts[row - 1, target, :BS, :] = value
            firsts[row - 1, target, BS:, :BS] = -value[:, BS:]
            firsts[row - 1, target, BS:, BS:] = value[:, :BS]

    assemble(recv, [0, 1], [2, 3], meta_ref)
    assemble(recv, [2], [4], meta_ref)
    first_row(3)

    whole_above = remote(above, above, fsend_sem.at[1], frecv_sem.at[1], nxt_id)
    whole_below = remote(below, below, fsend_sem.at[0], frecv_sem.at[0], prv_id)
    for copy in meta_copies:
        copy.wait_recv()
    whole_above.wait_recv()
    assemble(above, [0, 1], [0, 1], meta_up[2:6, :])
    first_row(1)
    first_row(2)
    whole_below.wait_recv()
    assemble(below, [0, 1], [5, 6], meta_down)
    first_row(4)
    first_row(5)

    for index in range(ROWS):
        row = index + 2
        results = []
        for target in range(3):
            second = product(row, target, firsts, 1)
            results.append(firsts[row - 1, target, :BS, :].astype(jnp.float32) - second)
        for slot in range(SLOTS):
            offset = meta_ref[2 * index + slot : 2 * index + slot + 1, :]
            for part in range(2):
                total = None
                for target in range(3):
                    term = jnp.where(
                        offset == float(target), results[target][:, part * BS : (part + 1) * BS], 0.0
                    )
                    total = term if total is None else total + term
                out_ref[0, part, index, slot] = total.astype(jnp.bfloat16)

    sent = recv.at[pl.ds(0, freqs - 1)]
    remote(sent, sent, send_sem, recv_sem.at[0], prv_id).wait_send()
    whole_above.wait_send()
    whole_below.wait_send()
    for copy in meta_copies:
        copy.wait_send()


def solution(mesh):
    freqs, srows, rcols = mesh.shape["freq"], mesh.shape["srow"], mesh.shape["rcol"]

    def per_device(data_time, block_cols, row_counts):
        samples = data_time.shape[-1]
        pairs = ROWS * SLOTS
        first_row = lax.axis_index(("srow", "rcol")) * ROWS
        row_index = first_row + jnp.arange(ROWS, dtype=jnp.int32)
        live = jnp.arange(SLOTS, dtype=jnp.int32)[None, :] < row_counts[:, None]
        offsets = jnp.where(live, block_cols - row_index[:, None] + 1, -1)
        meta = jnp.broadcast_to(offsets.astype(jnp.float32).reshape(pairs, 1), (pairs, BS))
        meta = jnp.concatenate([meta, jnp.full((8 - pairs, BS), -1.0, jnp.float32)], axis=0)
        table = jnp.asarray(spectral_table(samples, freqs))
        return pl.pallas_call(
            functools.partial(kernel, freqs, srows, rcols),
            out_shape=jax.ShapeDtypeStruct((1, 2, ROWS, SLOTS, BS, BS), jnp.bfloat16),
            in_specs=[
                pl.BlockSpec(memory_space=pl.ANY),
                pl.BlockSpec(memory_space=pl.ANY),
                pl.BlockSpec(memory_space=pltpu.VMEM),
            ],
            out_specs=pl.BlockSpec(memory_space=pltpu.VMEM),
            scratch_shapes=[
                pltpu.VMEM((pairs, PAIR, samples), jnp.bfloat16),
                pltpu.VMEM((2 * freqs, samples), jnp.bfloat16),
                pltpu.VMEM((freqs * ROWS * 8, BS), jnp.float32),
                pltpu.VMEM((freqs, ROWS, 8, BS), jnp.bfloat16),
                pltpu.VMEM((freqs, ROWS, 8, BS), jnp.bfloat16),
                pltpu.VMEM((freqs, 2, 8, BS), jnp.bfloat16),
                pltpu.VMEM((freqs, 2, 8, BS), jnp.bfloat16),
                pltpu.VMEM((8, BS), jnp.float32),
                pltpu.VMEM((8, BS), jnp.float32),
                pltpu.VMEM((8 * freqs, 8 * freqs), jnp.bfloat16),
                pltpu.VMEM((7, 3, PAIR, PAIR), jnp.bfloat16),
                pltpu.VMEM((5, 3, PAIR, PAIR), jnp.bfloat16),
                pltpu.SemaphoreType.DMA((pairs,)),
                pltpu.SemaphoreType.DMA,
                pltpu.SemaphoreType.DMA,
                pltpu.SemaphoreType.DMA,
                pltpu.SemaphoreType.DMA((freqs // GROUP,)),
                pltpu.SemaphoreType.DMA((2,)),
                pltpu.SemaphoreType.DMA((2,)),
                pltpu.SemaphoreType.DMA((2,)),
                pltpu.SemaphoreType.DMA((2,)),
            ],
            compiler_params=pltpu.CompilerParams(
                collective_id=0, has_side_effects=True, vmem_limit_bytes=40 * 1024 * 1024
            ),
        )(data_time.reshape(pairs, PAIR, samples), table, meta)

    return jax.shard_map(
        per_device,
        mesh=mesh,
        in_specs=(
            P(("srow", "rcol"), None, "freq", None, None),
            P(("srow", "rcol"), None),
            P(("srow", "rcol")),
        ),
        out_specs=P("freq", None, ("srow", "rcol"), None, None, None),
        check_vma=False,
    )
```

```python
import functools
import math

import jax
import jax.numpy as jnp
import numpy as np
from jax import lax
from jax.experimental import pallas as pl
from jax.experimental.pallas import tpu as pltpu
from jax.sharding import PartitionSpec as P

BS = 128
PAIR = 2 * BS
ROWS = 3
SLOTS = 2
MESH = pl.DeviceIdType.MESH


def spectral_table(samples, freq_count):
    time_index = np.arange(samples, dtype=np.int64)
    freq_bins = np.arange(freq_count, dtype=np.int64) + 1
    phase_int = freq_bins[:, None] * time_index[None, :] % samples
    angles = phase_int.astype(np.float32) * np.float32(2.0 * math.pi / samples)
    table = np.concatenate([np.cos(angles), -np.sin(angles)], axis=0)
    return (table * np.float32(1.0 / math.sqrt(samples))).astype(jnp.bfloat16)


def kernel(
    freqs, srows, rcols, order, batches, plan,
    x_hbm, table_hbm, cols_hbm, counts_hbm, out_ref,
    xv, tv, cols_ref, counts_ref, meta_ref, spread, sendbuf, recv, above, below, meta_up, meta_down, gather, bands, firsts,
    load_sem, table_sem, index_sem, own_sem, ready_sem, send_sem, recv_sem, fsend_sem, frecv_sem, msend_sem, mrecv_sem,
):
    chips = freqs // 2
    me = lax.axis_index("freq")
    zpos, core = me // 2, me % 2
    grow = lax.axis_index("srow") * rcols + lax.axis_index("rcol")
    groups = srows * rcols
    nxt, prv = (grow + 1) % groups, (grow + groups - 1) % groups
    nxt_id = (me, nxt // rcols, nxt % rcols)
    prv_id = (me, prv // rcols, prv % rcols)
    pairs = ROWS * SLOTS

    table_copy = pltpu.make_async_copy(table_hbm, tv, table_sem)
    table_copy.start()
    loads = [pltpu.make_async_copy(x_hbm.at[n], xv.at[n], load_sem.at[n]) for n in range(pairs)]
    for load in loads:
        load.start()

    index_copies = [
        pltpu.make_async_copy(cols_hbm, cols_ref, index_sem.at[0]),
        pltpu.make_async_copy(counts_hbm, counts_ref, index_sem.at[1]),
    ]
    for copy in index_copies:
        copy.start()

    near = chips // 4
    barrier = pltpu.get_barrier_semaphore()
    for reach in range(near, -1, -1):
        for way in (1, -1):
            chip = (zpos + chips + way * reach) % chips
            for other in range(2):
                if reach or (way, other) == (1, 0):
                    pl.semaphore_signal(
                        barrier,
                        inc=1,
                        device_id={"freq": 2 * chip + (other if reach else 1 - core)},
                        device_id_type=MESH,
                    )
    pl.semaphore_signal(barrier, inc=1, device_id=nxt_id, device_id_type=MESH)
    pl.semaphore_signal(barrier, inc=1, device_id=prv_id, device_id_type=MESH)

    table_copy.wait()
    for n in range(pairs):
        loads[n].wait()
        row, slot = n // SLOTS, n % SLOTS
        value = lax.dot_general(
            tv[...], xv[n], (((1,), (1,)), ((), ())), preferred_element_type=jnp.float32
        )
        for part in range(2):
            for trace in range(2):
                place = row * 8 + part * 4 + slot * 2 + trace
                spread[pl.ds(place, freqs, stride=ROWS * 8), :] = value[
                    part * freqs : (part + 1) * freqs, trace * BS : (trace + 1) * BS
                ]
    sendbuf[...] = spread[...].reshape(freqs, ROWS, 8, BS).astype(jnp.bfloat16)

    for copy in index_copies:
        copy.wait()
    for row in range(ROWS):
        for slot in range(SLOTS):
            offset = cols_ref[slot : slot + 1, row : row + 1] - (ROWS * grow + row) + 1
            offset = jnp.where(counts_ref[:, row : row + 1] > slot, offset, -1)
            meta_ref[2 * row + slot : 2 * row + slot + 1, :] = jnp.broadcast_to(
                offset.astype(jnp.float32), (1, BS)
            )
    meta_ref[pairs:, :] = jnp.full((8 - pairs, BS), -1.0, jnp.float32)

    def remote(src, dst, ssem, rsem, target):
        return pltpu.make_async_remote_copy(
            src_ref=src, dst_ref=dst, send_sem=ssem, recv_sem=rsem,
            device_id=target, device_id_type=MESH,
        )

    def send(place):
        chip = (zpos + chips + order[place]) % chips
        batch = [low <= place < high for low, high in batches].index(True)
        for other in range(2):
            target = 2 * chip + (other if order[place] else 1 - core)
            if order[place] or other == 0:
                remote(
                    sendbuf.at[target], recv.at[2 * place + core], send_sem, recv_sem.at[batch],
                    {"freq": target},
                ).start()

    arrival = lax.broadcasted_iota(jnp.int32, (1, 8 * freqs), 1)
    came = jnp.zeros_like(arrival)
    for place, chip in enumerate(order):
        came = jnp.where(arrival >> 4 == place, chip, came)
    origin = ((zpos + chips - came) & (chips - 1)) * 2 + ((arrival >> 3) & 1)
    key_in = origin * 8 + (arrival & 7)
    place = lax.broadcasted_iota(jnp.int32, (8 * freqs, 1), 0)
    trace_index = place & (BS - 1)
    key_out = (
        (trace_index >> 1) * 8
        + ((place >> 7) & 1) * 4
        + ((place >> 8) & 1) * 2
        + (trace_index & 1)
    )
    gather[...] = jnp.where(key_in == key_out, 1.0, 0.0).astype(jnp.bfloat16)

    def relay(batch):
        low, high = batches[batch]
        mine = low <= home < high
        low, high = 2 * low, 2 * high
        arrived = recv.at[pl.ds(low, high - low - mine)]
        remote(arrived, arrived, send_sem, recv_sem.at[batch], prv_id).wait_recv()
        if mine:
            own_copy.wait()
        span = pl.ds(low, high - low)
        remote(
            recv.at[span, pl.ds(0, 2)], below.at[span], fsend_sem.at[0], frecv_sem.at[0], prv_id
        ).start()
        remote(
            recv.at[span, pl.ds(1, 2)], above.at[span], fsend_sem.at[1], frecv_sem.at[1], nxt_id
        ).start()

    pl.semaphore_wait(barrier, 4 * near + 3)
    home = order.index(0)
    own_copy = pltpu.make_async_copy(sendbuf.at[me], recv.at[2 * home + core], own_sem)
    own_copy.start()
    for way in (1, chips - 1):
        pl.semaphore_signal(
            ready_sem,
            inc=1,
            device_id={"freq": 2 * ((zpos + way * near) % chips) + core},
            device_id_type=MESH,
        )
    meta_copies = [
        remote(meta_ref, meta_up, msend_sem.at[0], mrecv_sem.at[0], nxt_id),
        remote(meta_ref, meta_down, msend_sem.at[1], mrecv_sem.at[1], prv_id),
    ]
    for copy in meta_copies:
        copy.start()
    for kind, value in plan:
        if kind == "send":
            for place in range(*batches[value]):
                send(place)
        elif kind == "relay":
            relay(value)
        else:
            pl.semaphore_wait(ready_sem, 2)

    def rows_of(ref, index):
        return ref[:, index].astype(jnp.float32).reshape(8 * freqs, BS).astype(jnp.bfloat16)

    def place_band(row, block, offsets):
        for shift in range(3):
            parts = []
            for part in range(2):
                total = None
                for slot in range(SLOTS):
                    first = slot * PAIR + part * BS
                    live = jnp.where(offsets[slot] == float(shift), block[first : first + BS], 0.0)
                    total = live if total is None else total + live
                parts.append(total)
            bands[row, shift, :BS, :BS] = parts[0].astype(jnp.bfloat16)
            bands[row, shift, :BS, BS:] = parts[1].astype(jnp.bfloat16)
            bands[row, shift, BS:, :BS] = (-parts[1]).astype(jnp.bfloat16)
            bands[row, shift, BS:, BS:] = parts[0].astype(jnp.bfloat16)

    def assemble(ref, indices, rows, meta):
        stacked = [rows_of(ref, index) for index in indices]
        joined = stacked[0] if len(stacked) == 1 else jnp.concatenate(stacked, axis=1)
        blocks = jnp.dot(gather[...], joined, preferred_element_type=jnp.float32)
        for n, (index, row) in enumerate(zip(indices, rows)):
            offsets = [meta[2 * index + slot : 2 * index + slot + 1, :] for slot in range(SLOTS)]
            place_band(row, blocks[:, n * BS : (n + 1) * BS], offsets)

    scale = (3.0 * BS) ** (-0.5)

    def product(row, target, right, shift_row):
        total = None
        for source in range(3):
            inner = target - source + 1
            if 0 <= inner <= 2:
                term = jnp.dot(
                    bands[row, source, :BS, :],
                    right[row + source - 1 - shift_row, inner],
                    preferred_element_type=jnp.float32,
                )
                total = term if total is None else total + term
        return total * scale

    def first_row(row):
        for target in range(3):
            value = product(row, target, bands, 0).astype(jnp.bfloat16)
            firsts[row - 1, target, :BS, :] = value
            firsts[row - 1, target, BS:, :BS] = -value[:, BS:]
            firsts[row - 1, target, BS:, BS:] = value[:, :BS]

    assemble(recv, [0, 1], [2, 3], meta_ref)
    assemble(recv, [2], [4], meta_ref)
    first_row(3)

    whole_above = remote(above, above, fsend_sem.at[1], frecv_sem.at[1], nxt_id)
    whole_below = remote(below, below, fsend_sem.at[0], frecv_sem.at[0], prv_id)
    for copy in meta_copies:
        copy.wait_recv()
    whole_above.wait_recv()
    assemble(above, [0, 1], [0, 1], meta_up[2:6, :])
    first_row(1)
    first_row(2)
    whole_below.wait_recv()
    assemble(below, [0, 1], [5, 6], meta_down)
    first_row(4)
    first_row(5)

    for index in range(ROWS):
        row = index + 2
        results = []
        for target in range(3):
            second = product(row, target, firsts, 1)
            results.append(firsts[row - 1, target, :BS, :].astype(jnp.float32) - second)
        for slot in range(SLOTS):
            offset = meta_ref[2 * index + slot : 2 * index + slot + 1, :]
            for part in range(2):
                total = None
                for target in range(3):
                    term = jnp.where(
                        offset == float(target), results[target][:, part * BS : (part + 1) * BS], 0.0
                    )
                    total = term if total is None else total + term
                out_ref[0, part, index, slot] = total.astype(jnp.bfloat16)

    sent = recv.at[pl.ds(0, freqs - 1)]
    remote(sent, sent, send_sem, recv_sem.at[0], prv_id).wait_send()
    whole_above.wait_send()
    whole_below.wait_send()
    for copy in meta_copies:
        copy.wait_send()


def schedule(chips):
    def both(*reaches):
        return [step for reach in reaches for step in (reach, -reach)]

    groups = [
        both(8, 7, 6),
        both(5, 4) + [0],
        [16] + both(15, 14),
        both(13, 12, 11),
        both(10, 9),
        both(3, 2, 1),
    ]
    order = [step for group in groups for step in group]
    cuts = [sum(len(group) for group in groups[:n]) for n in range(len(groups) + 1)]
    batches = list(zip(cuts[:-1], cuts[1:]))
    plan = [
        ("send", 0), ("send", 1), ("ready", 0), ("send", 2), ("send", 3), ("relay", 0), ("relay", 1),
        ("send", 4), ("relay", 2), ("send", 5), ("relay", 3), ("relay", 4), ("relay", 5),
    ]
    return order, batches, plan


def solution(mesh):
    freqs, srows, rcols = mesh.shape["freq"], mesh.shape["srow"], mesh.shape["rcol"]

    def per_device(data_time, block_cols, row_counts):
        samples = data_time.shape[-1]
        pairs = ROWS * SLOTS
        chips = freqs // 2
        order, batches, plan = schedule(chips)
        table = jnp.asarray(spectral_table(samples, freqs))
        return pl.pallas_call(
            functools.partial(kernel, freqs, srows, rcols, order, batches, plan),
            out_shape=jax.ShapeDtypeStruct((1, 2, ROWS, SLOTS, BS, BS), jnp.bfloat16),
            in_specs=[
                pl.BlockSpec(memory_space=pl.ANY),
                pl.BlockSpec(memory_space=pl.ANY),
                pl.BlockSpec(memory_space=pl.ANY),
                pl.BlockSpec(memory_space=pl.ANY),
            ],
            out_specs=pl.BlockSpec(memory_space=pltpu.VMEM),
            scratch_shapes=[
                pltpu.VMEM((pairs, PAIR, samples), jnp.bfloat16),
                pltpu.VMEM((2 * freqs, samples), jnp.bfloat16),
                pltpu.VMEM((SLOTS, ROWS), jnp.int32),
                pltpu.VMEM((1, ROWS), jnp.int32),
                pltpu.VMEM((8, BS), jnp.float32),
                pltpu.VMEM((freqs * ROWS * 8, BS), jnp.float32),
                pltpu.VMEM((freqs, ROWS, 8, BS), jnp.bfloat16),
                pltpu.VMEM((freqs, ROWS, 8, BS), jnp.bfloat16),
                pltpu.VMEM((freqs, 2, 8, BS), jnp.bfloat16),
                pltpu.VMEM((freqs, 2, 8, BS), jnp.bfloat16),
                pltpu.VMEM((8, BS), jnp.float32),
                pltpu.VMEM((8, BS), jnp.float32),
                pltpu.VMEM((8 * freqs, 8 * freqs), jnp.bfloat16),
                pltpu.VMEM((7, 3, PAIR, PAIR), jnp.bfloat16),
                pltpu.VMEM((5, 3, PAIR, PAIR), jnp.bfloat16),
                pltpu.SemaphoreType.DMA((pairs,)),
                pltpu.SemaphoreType.DMA,
                pltpu.SemaphoreType.DMA((2,)),
                pltpu.SemaphoreType.DMA,
                pltpu.SemaphoreType.REGULAR,
                pltpu.SemaphoreType.DMA,
                pltpu.SemaphoreType.DMA((len(batches),)),
                pltpu.SemaphoreType.DMA((2,)),
                pltpu.SemaphoreType.DMA((2,)),
                pltpu.SemaphoreType.DMA((2,)),
                pltpu.SemaphoreType.DMA((2,)),
            ],
            compiler_params=pltpu.CompilerParams(
                collective_id=0, has_side_effects=True, vmem_limit_bytes=60 * 1024 * 1024
            ),
        )(
            data_time.reshape(pairs, PAIR, samples),
            table,
            block_cols.T,
            row_counts.reshape(1, ROWS),
        )

    return jax.shard_map(
        per_device,
        mesh=mesh,
        in_specs=(
            P(("srow", "rcol"), None, "freq", None, None),
            P(("srow", "rcol"), None),
            P(("srow", "rcol")),
        ),
        out_specs=P("freq", None, ("srow", "rcol"), None, None, None),
        check_vma=False,
    )
```

```python
import functools
import math

import jax
import jax.numpy as jnp
from jax import lax
from jax.experimental import pallas as pl
from jax.experimental.pallas import tpu as pltpu
from jax.sharding import PartitionSpec as P

BS = 128
PAIR = 2 * BS
ROWS = 3
SLOTS = 2
MESH = pl.DeviceIdType.MESH


def spectral_table(samples, freqs):
    row = lax.broadcasted_iota(jnp.int32, (2 * freqs, samples), 0)
    time = lax.broadcasted_iota(jnp.int32, (2 * freqs, samples), 1)
    part = (row >= freqs).astype(jnp.int32)
    phase = ((row - part * freqs + 1) * time + part * (samples // 4)) & (samples - 1)
    folded = jnp.abs(phase - samples // 2) - samples // 4
    angle = folded.astype(jnp.float32) * (2.0 * math.pi / samples)
    square = angle * angle
    value = jnp.full_like(square, -1.0 / math.factorial(11))
    for power in (9, 7, 5, 3, 1):
        value = value * square + (-1.0) ** (power // 2) / math.factorial(power)
    return (value * angle * (1.0 / math.sqrt(samples))).astype(jnp.bfloat16)


def kernel(
    freqs, srows, rcols, order, batches, plan, hops,
    x_hbm, cols_ref, out_ref,
    xv, tv, meta_ref, spread, sendbuf, recv, border, border_meta, gather, bands, firsts, partial, seconds,
    load_sem, own_sem, ready_sem, send_sem, recv_sem, fsend_sem, frecv_sem, msend_sem, mrecv_sem,
):
    chips = freqs // 2
    me = lax.axis_index("freq")
    zpos, core = me // 2, me % 2
    grow = lax.axis_index("srow") * rcols + lax.axis_index("rcol")
    groups = srows * rcols
    nxt, prv = (grow + 1) % groups, (grow + groups - 1) % groups
    has_nxt, has_prv = grow < groups - 1, grow > 0
    nxt_id = (me, nxt // rcols, nxt % rcols)
    prv_id = (me, prv // rcols, prv % rcols)
    pairs = ROWS * SLOTS
    home = order.index(0)

    loads = [pltpu.make_async_copy(x_hbm.at[n], xv.at[n], load_sem.at[n]) for n in range(pairs)]
    for load in loads:
        load.start()

    near, further = hops
    barrier = pltpu.get_barrier_semaphore()
    for reach in range(near, -1, -1):
        for way in (1, -1):
            chip = (zpos + chips + way * reach) % chips
            for other in range(2):
                if reach or (way, other) == (1, 0):
                    pl.semaphore_signal(
                        barrier,
                        inc=1,
                        device_id={"freq": 2 * chip + (other if reach else 1 - core)},
                        device_id_type=MESH,
                    )
    pl.semaphore_signal(barrier, inc=1, device_id=nxt_id, device_id_type=MESH)
    pl.semaphore_signal(barrier, inc=1, device_id=prv_id, device_id_type=MESH)

    tv[...] = spectral_table(tv.shape[1], freqs)
    for n in range(pairs):
        loads[n].wait()
        row, slot = n // SLOTS, n % SLOTS
        value = lax.dot_general(
            tv[...], xv[n], (((1,), (1,)), ((), ())), preferred_element_type=jnp.float32
        )
        for part in range(2):
            for trace in range(2):
                place = row * 8 + part * 4 + slot * 2 + trace
                spread[pl.ds(place, freqs, stride=ROWS * 8), :] = value[
                    part * freqs : (part + 1) * freqs, trace * BS : (trace + 1) * BS
                ]
    sendbuf[...] = spread[: freqs * ROWS * 8, :].reshape(freqs, ROWS, 8, BS).astype(jnp.bfloat16)

    for row in range(ROWS):
        for slot in range(SLOTS):
            offset = cols_ref[slot : slot + 1, row : row + 1] - (ROWS * grow + row) + 1
            meta_ref[2 * row + slot : 2 * row + slot + 1, :] = jnp.broadcast_to(
                offset.astype(jnp.float32), (1, BS)
            )
    meta_ref[pairs:, :] = jnp.full((8 - pairs, BS), -1.0, jnp.float32)

    def remote(src, dst, ssem, rsem, target):
        return pltpu.make_async_remote_copy(
            src_ref=src, dst_ref=dst, send_sem=ssem, recv_sem=rsem,
            device_id=target, device_id_type=MESH,
        )

    def send(place):
        chip = (zpos + chips + order[place]) % chips
        batch = [low <= place < high for low, high in batches].index(True)
        for other in range(2):
            target = 2 * chip + (other if order[place] else 1 - core)
            if order[place] or other == 0:
                remote(
                    sendbuf.at[target], recv.at[2 * place + core], send_sem.at[batch], recv_sem.at[batch],
                    {"freq": target},
                ).start()

    arrival = lax.broadcasted_iota(jnp.int32, (1, 8 * freqs), 1)
    came = jnp.zeros_like(arrival)
    for place, chip in enumerate(order):
        came = jnp.where(arrival >> 4 == place, chip, came)
    origin = ((zpos + chips - came) & (chips - 1)) * 2 + ((arrival >> 3) & 1)
    key_in = origin * 8 + (arrival & 7)
    place = lax.broadcasted_iota(jnp.int32, (8 * freqs, 1), 0)
    trace_index = place & (BS - 1)
    key_out = (
        (trace_index >> 1) * 8
        + ((place >> 7) & 1) * 4
        + ((place >> 8) & 1) * 2
        + (trace_index & 1)
    )
    gather[...] = jnp.where(key_in == key_out, 1.0, 0.0).astype(jnp.bfloat16)

    def sent(batch):
        low, high = batches[batch]
        span = recv.at[pl.ds(2 * low, 2 * (high - low) - (low <= home < high))]
        remote(span, span, send_sem.at[batch], recv_sem.at[batch], prv_id).wait_send()

    def relay(batch):
        low, high = batches[batch]
        mine = low <= home < high
        low, high = 2 * low, 2 * high
        arrived = recv.at[pl.ds(low, high - low - mine)]
        remote(arrived, arrived, send_sem.at[batch], recv_sem.at[batch], prv_id).wait_recv()
        if mine:
            own_copy.wait()
        span = pl.ds(low, high - low)
        down = remote(
            recv.at[span, pl.ds(0, 2)], border.at[1, span], fsend_sem.at[1], frecv_sem.at[1], prv_id
        )
        up = remote(
            recv.at[span, pl.ds(1, 2)], border.at[0, span], fsend_sem.at[0], frecv_sem.at[0], nxt_id
        )
        pl.when(has_prv)(down.start)
        pl.when(has_nxt)(up.start)

    def announce():
        for way in (1, chips - 1):
            pl.semaphore_signal(
                ready_sem,
                inc=1,
                device_id={"freq": 2 * ((zpos + way * further) % chips) + core},
                device_id_type=MESH,
            )

    for side, there in enumerate((has_prv, has_nxt)):

        @pl.when(jnp.logical_not(there))
        def _(side=side):
            border[side] = jnp.zeros(border.shape[1:], border.dtype)
            border_meta[side] = jnp.full(border_meta.shape[1:], -1.0, border_meta.dtype)

    pl.semaphore_wait(barrier, 4 * near + 3)
    own_copy = pltpu.make_async_copy(sendbuf.at[me], recv.at[2 * home + core], own_sem)
    own_copy.start()
    announce()
    meta_copies = [
        remote(meta_ref, border_meta.at[0], msend_sem.at[0], mrecv_sem.at[0], nxt_id),
        remote(meta_ref, border_meta.at[1], msend_sem.at[1], mrecv_sem.at[1], prv_id),
    ]
    pl.when(has_nxt)(meta_copies[0].start)
    pl.when(has_prv)(meta_copies[1].start)
    for kind, value in plan:
        if kind == "send":
            for place in range(*batches[value]):
                send(place)
        elif kind == "relay":
            relay(value)
        elif kind == "sent":
            sent(value)
        else:
            pl.semaphore_wait(ready_sem, 2)

    def rows_of(part):
        return part.astype(jnp.float32).reshape(8 * freqs, BS).astype(jnp.bfloat16)

    def place_band(row, block, offsets):
        for shift in range(3):
            parts = []
            for part in range(2):
                total = None
                for slot in range(SLOTS):
                    first = slot * PAIR + part * BS
                    live = jnp.where(offsets[slot] == float(shift), block[first : first + BS], 0.0)
                    total = live if total is None else total + live
                parts.append(total)
            bands[row, shift, :BS, :BS] = parts[0].astype(jnp.bfloat16)
            bands[row, shift, :BS, BS:] = parts[1].astype(jnp.bfloat16)
            bands[row, shift, BS:, :BS] = (-parts[1]).astype(jnp.bfloat16)
            bands[row, shift, BS:, BS:] = parts[0].astype(jnp.bfloat16)

    def assemble(rows, offsets, first):
        joined = jnp.concatenate([rows_of(row) for row in rows], axis=1)
        blocks = jnp.dot(gather[...], joined, preferred_element_type=jnp.float32)
        for n in range(len(rows)):
            place_band(first + n, blocks[:, n * BS : (n + 1) * BS], offsets[n])

    scale = (3.0 * BS) ** (-0.5)

    def band_term(row, source, inner):
        return jnp.dot(
            bands[row, source, :BS, :], bands[row + source - 1, inner],
            preferred_element_type=jnp.float32,
        )

    def first_term(row, source, inner):
        return jnp.dot(
            bands[row, source, :BS, :], firsts[row + source - 2, inner],
            preferred_element_type=jnp.float32,
        )

    def keep_first(row, target, total):
        value = (total * scale).astype(jnp.bfloat16)
        firsts[row - 1, target, :BS, :] = value
        firsts[row - 1, target, BS:, :BS] = -value[:, BS:]
        firsts[row - 1, target, BS:, BS:] = value[:, :BS]

    def total_of(term, row, target, sources):
        terms = [
            term(row, source, target - source + 1)
            for source in sources
            if 0 <= target - source + 1 <= 2
        ]
        return sum(terms[1:], terms[0]) if terms else jnp.zeros((BS, PAIR), jnp.float32)

    def finish(index):
        results = [
            firsts[index + 1, target, :BS, :].astype(jnp.float32) - seconds[index, target] * scale
            for target in range(3)
        ]
        for slot in range(SLOTS):
            offset = meta_ref[pl.ds(2 * index + slot, 1), :]
            for part in range(2):
                span = slice(part * BS, (part + 1) * BS)
                chosen = [
                    jnp.where(offset == float(target), results[target][:, span], 0.0)
                    for target in range(3)
                ]
                out_ref[0, part, index, slot] = (chosen[0] + chosen[1] + chosen[2]).astype(jnp.bfloat16)

    own_offsets = [
        [meta_ref[2 * n + slot : 2 * n + slot + 1, :] for slot in range(SLOTS)] for n in range(ROWS)
    ]
    assemble([recv[:, 0], recv[:, 1]], own_offsets[:2], 2)
    assemble([recv[:, 2]], own_offsets[2:], 4)
    for target in range(3):
        keep_first(3, target, total_of(band_term, 3, target, range(3)))
        partial[0, target] = total_of(band_term, 2, target, (1, 2))
        partial[1, target] = total_of(band_term, 4, target, (0, 1))
    for target in range(3):
        seconds[0, target] = total_of(first_term, 2, target, (2,))
        seconds[1, target] = total_of(first_term, 3, target, (1,))
        seconds[2, target] = total_of(first_term, 4, target, (0,))

    for side, there in ((1, has_nxt), (0, has_prv)):

        @pl.when(there)
        def _(side=side):
            mine, whole = border_meta.at[side], border.at[side]
            remote(mine, mine, msend_sem.at[side], mrecv_sem.at[side], prv_id).wait_recv()
            remote(whole, whole, fsend_sem.at[side], frecv_sem.at[side], prv_id).wait_recv()

        lines = [2 * n + 2 - 2 * side for n in range(2)]
        offsets = [
            [border_meta[side, line + slot : line + slot + 1, :] for slot in range(SLOTS)]
            for line in lines
        ]
        assemble([border[side, :, 0], border[side, :, 1]], offsets, 5 * side)
    for side in range(2):
        outer, inner = 1 + 4 * side, 2 + 2 * side
        for target in (1 - side, 2 - side):
            keep_first(outer, target, total_of(band_term, outer, target, range(3)))
        for target in range(3):
            keep_first(
                inner, target,
                partial[side, target] + total_of(band_term, inner, target, (2 * side,)),
            )
    for side in range(2):
        inner = 2 + 2 * side
        for target in range(3):
            seconds[2 * side, target] += total_of(first_term, inner, target, (2 * side, 1))
        finish(2 * side)
    for target in range(3):
        seconds[1, target] += total_of(first_term, 3, target, (0, 2))
    finish(1)

    for batch in range(len(batches)):
        if ("sent", batch) not in plan:
            sent(batch)
    for side, there in enumerate((has_nxt, has_prv)):

        @pl.when(there)
        def _(side=side):
            whole = border.at[side]
            remote(whole, whole, fsend_sem.at[side], frecv_sem.at[side], prv_id).wait_send()
            meta_copies[side].wait_send()


def schedule(chips):
    def both(*reaches):
        return [step for reach in reaches for step in (reach, -reach)]

    groups = [both(8,7), both(6)+[0], [16]+both(15,14), both(13,12,11), both(10,9), both(5,4,3), both(2,1)]
    order = [step for group in groups for step in group]
    cuts = [sum(len(group) for group in groups[:n]) for n in range(len(groups) + 1)]
    batches = list(zip(cuts[:-1], cuts[1:]))
    hops = (8, 8)
    plan = [('send', 0), ('send', 1), ('ready', 0), ('send', 2), ('send', 3), ('relay', 0), ('relay', 1), ('send', 4), ('relay', 2), ('send', 5), ('send', 6), ('relay', 3), ('relay', 4), ('relay', 5), ('relay', 6)]
    return order, batches, plan, hops


def solution(mesh):
    freqs, srows, rcols = mesh.shape["freq"], mesh.shape["srow"], mesh.shape["rcol"]

    def per_device(data_time, block_cols, row_counts):
        samples = data_time.shape[-1]
        pairs = ROWS * SLOTS
        chips = freqs // 2
        order, batches, plan, hops = schedule(chips)
        live = jnp.arange(SLOTS, dtype=jnp.int32)[:, None] < row_counts[None, :]
        cols = jnp.where(live, block_cols.T, -1000)
        return pl.pallas_call(
            functools.partial(kernel, freqs, srows, rcols, order, batches, plan, hops),
            out_shape=jax.ShapeDtypeStruct((1, 2, ROWS, SLOTS, BS, BS), jnp.bfloat16),
            in_specs=[
                pl.BlockSpec(memory_space=pl.ANY),
                pl.BlockSpec(memory_space=pltpu.VMEM),
            ],
            out_specs=pl.BlockSpec(memory_space=pltpu.VMEM),
            scratch_shapes=[
                pltpu.VMEM((pairs, PAIR, samples), jnp.bfloat16),
                pltpu.VMEM((2 * freqs, samples), jnp.bfloat16),
                pltpu.VMEM((8, BS), jnp.float32),
                pltpu.VMEM(((freqs + 1) * ROWS * 8, BS), jnp.float32),
                pltpu.VMEM((freqs, ROWS, 8, BS), jnp.bfloat16),
                pltpu.VMEM((freqs, ROWS, 8, BS), jnp.bfloat16),
                pltpu.VMEM((2, freqs, 2, 8, BS), jnp.bfloat16),
                pltpu.VMEM((2, 8, BS), jnp.float32),
                pltpu.VMEM((8 * freqs, 8 * freqs), jnp.bfloat16),
                pltpu.VMEM((7, 3, PAIR, PAIR), jnp.bfloat16),
                pltpu.VMEM((5, 3, PAIR, PAIR), jnp.bfloat16),
                pltpu.VMEM((2, 3, BS, PAIR), jnp.float32),
                pltpu.VMEM((ROWS, 3, BS, PAIR), jnp.float32),
                pltpu.SemaphoreType.DMA((pairs,)),
                pltpu.SemaphoreType.DMA,
                pltpu.SemaphoreType.REGULAR,
                pltpu.SemaphoreType.DMA((len(batches),)),
                pltpu.SemaphoreType.DMA((len(batches),)),
                pltpu.SemaphoreType.DMA((2,)),
                pltpu.SemaphoreType.DMA((2,)),
                pltpu.SemaphoreType.DMA((2,)),
                pltpu.SemaphoreType.DMA((2,)),
            ],
            compiler_params=pltpu.CompilerParams(
                collective_id=0, has_side_effects=True, vmem_limit_bytes=55574528
            ),
        )(
            data_time.reshape(pairs, PAIR, samples),
            cols,
        )

    return jax.shard_map(
        per_device,
        mesh=mesh,
        in_specs=(
            P(("srow", "rcol"), None, "freq", None, None),
            P(("srow", "rcol"), None),
            P(("srow", "rcol")),
        ),
        out_specs=P("freq", None, ("srow", "rcol"), None, None, None),
        check_vma=False,
    )
```

```python
import functools
import math

import jax
import jax.numpy as jnp
from jax import lax
from jax.experimental import pallas as pl
from jax.experimental.pallas import tpu as pltpu
from jax.sharding import PartitionSpec as P

BS = 128
PAIR = 2 * BS
ROWS = 3
SLOTS = 2
MESH = pl.DeviceIdType.MESH


def spectral_table(samples, freqs):
    row = lax.broadcasted_iota(jnp.int32, (2 * freqs, samples), 0)
    time = lax.broadcasted_iota(jnp.int32, (2 * freqs, samples), 1)
    part = (row >= freqs).astype(jnp.int32)
    phase = ((row - part * freqs + 1) * time + part * (samples // 4)) & (samples - 1)
    folded = jnp.abs(phase - samples // 2) - samples // 4
    angle = folded.astype(jnp.float32) * (2.0 * math.pi / samples)
    square = angle * angle
    value = jnp.full_like(square, -1.0 / math.factorial(11))
    for power in (9, 7, 5, 3, 1):
        value = value * square + (-1.0) ** (power // 2) / math.factorial(power)
    return (value * angle * (1.0 / math.sqrt(samples))).astype(jnp.bfloat16)


def kernel(
    freqs, srows, rcols, order, batches, plan, hops,
    x_hbm, cols_hbm, counts_hbm, out_ref,
    xv, tv, cols_ref, counts_ref, meta_ref, spread, sendbuf, recv, border, border_meta, gather, bands, firsts, partial, seconds,
    load_sem, index_sem, own_sem, ready_sem, send_sem, recv_sem, fsend_sem, frecv_sem, msend_sem, mrecv_sem,
):
    chips = freqs // 2
    me = lax.axis_index("freq")
    zpos, core = me // 2, me % 2
    grow = lax.axis_index("srow") * rcols + lax.axis_index("rcol")
    groups = srows * rcols
    nxt, prv = (grow + 1) % groups, (grow + groups - 1) % groups
    has_nxt, has_prv = grow < groups - 1, grow > 0
    nxt_id = (me, nxt // rcols, nxt % rcols)
    prv_id = (me, prv // rcols, prv % rcols)
    pairs = ROWS * SLOTS
    home = order.index(0)

    loads = [pltpu.make_async_copy(x_hbm.at[n], xv.at[n], load_sem.at[n]) for n in range(pairs)]
    index_copies = [
        pltpu.make_async_copy(cols_hbm, cols_ref, index_sem.at[0]),
        pltpu.make_async_copy(counts_hbm, counts_ref, index_sem.at[1]),
    ]
    for load in loads + index_copies:
        load.start()

    near, further = hops
    barrier = pltpu.get_barrier_semaphore()
    for reach in range(near, -1, -1):
        for way in (1, -1):
            chip = (zpos + chips + way * reach) % chips
            for other in range(2):
                if reach or (way, other) == (1, 0):
                    pl.semaphore_signal(
                        barrier,
                        inc=1,
                        device_id={"freq": 2 * chip + (other if reach else 1 - core)},
                        device_id_type=MESH,
                    )
    pl.semaphore_signal(barrier, inc=1, device_id=nxt_id, device_id_type=MESH)
    pl.semaphore_signal(barrier, inc=1, device_id=prv_id, device_id_type=MESH)

    tv[...] = spectral_table(tv.shape[1], freqs)
    for n in range(pairs):
        loads[n].wait()
        row, slot = n // SLOTS, n % SLOTS
        value = lax.dot_general(
            tv[...], xv[n], (((1,), (1,)), ((), ())), preferred_element_type=jnp.float32
        )
        for part in range(2):
            for trace in range(2):
                place = row * 8 + part * 4 + slot * 2 + trace
                spread[pl.ds(place, freqs, stride=ROWS * 8), :] = value[
                    part * freqs : (part + 1) * freqs, trace * BS : (trace + 1) * BS
                ]
    sendbuf[...] = spread[: freqs * ROWS * 8, :].reshape(freqs, ROWS, 8, BS).astype(jnp.bfloat16)

    for copy in index_copies:
        copy.wait()
    for row in range(ROWS):
        for slot in range(SLOTS):
            offset = cols_ref[slot : slot + 1, row : row + 1] - (ROWS * grow + row) + 1
            offset = jnp.where(counts_ref[:, row : row + 1] > slot, offset, -1)
            meta_ref[2 * row + slot : 2 * row + slot + 1, :] = jnp.broadcast_to(
                offset.astype(jnp.float32), (1, BS)
            )
    meta_ref[pairs:, :] = jnp.full((8 - pairs, BS), -1.0, jnp.float32)

    def remote(src, dst, ssem, rsem, target):
        return pltpu.make_async_remote_copy(
            src_ref=src, dst_ref=dst, send_sem=ssem, recv_sem=rsem,
            device_id=target, device_id_type=MESH,
        )

    def send(place):
        chip = (zpos + chips + (1 - 2 * core) * order[place]) % chips
        batch = [low <= place < high for low, high in batches].index(True)
        for other in range(2):
            target = 2 * chip + (other if order[place] else 1 - core)
            if order[place] or other == 0:
                remote(
                    sendbuf.at[target], recv.at[2 * place + core], send_sem.at[batch], recv_sem.at[batch],
                    {"freq": target},
                ).start()

    arrival = lax.broadcasted_iota(jnp.int32, (1, 8 * freqs), 1)
    came = jnp.zeros_like(arrival)
    for place, chip in enumerate(order):
        came = jnp.where(arrival >> 4 == place, chip, came)
    from_core = (arrival >> 3) & 1
    origin = ((zpos + chips - (1 - 2 * from_core) * came) & (chips - 1)) * 2 + from_core
    key_in = origin * 8 + (arrival & 7)
    place = lax.broadcasted_iota(jnp.int32, (8 * freqs, 1), 0)
    trace_index = place & (BS - 1)
    key_out = (
        (trace_index >> 1) * 8
        + ((place >> 7) & 1) * 4
        + ((place >> 8) & 1) * 2
        + (trace_index & 1)
    )
    gather[...] = jnp.where(key_in == key_out, 1.0, 0.0).astype(jnp.bfloat16)

    def sent(batch):
        low, high = batches[batch]
        span = recv.at[pl.ds(2 * low, 2 * (high - low) - (low <= home < high))]
        remote(span, span, send_sem.at[batch], recv_sem.at[batch], prv_id).wait_send()

    def relay(batch):
        low, high = batches[batch]
        mine = low <= home < high
        low, high = 2 * low, 2 * high
        arrived = recv.at[pl.ds(low, high - low - mine)]
        remote(arrived, arrived, send_sem.at[batch], recv_sem.at[batch], prv_id).wait_recv()
        if mine:
            own_copy.wait()
        span = pl.ds(low, high - low)
        down = remote(
            recv.at[span, pl.ds(0, 2)], border.at[1, span], fsend_sem.at[1], frecv_sem.at[1], prv_id
        )
        up = remote(
            recv.at[span, pl.ds(1, 2)], border.at[0, span], fsend_sem.at[0], frecv_sem.at[0], nxt_id
        )
        pl.when(has_nxt)(up.start)
        pl.when(has_prv)(down.start)

    def announce():
        for way in (1, chips - 1):
            pl.semaphore_signal(
                ready_sem,
                inc=1,
                device_id={"freq": 2 * ((zpos + way * further) % chips) + core},
                device_id_type=MESH,
            )

    for side, there in enumerate((has_prv, has_nxt)):

        @pl.when(jnp.logical_not(there))
        def _(side=side):
            border[side] = jnp.zeros(border.shape[1:], border.dtype)
            border_meta[side] = jnp.full(border_meta.shape[1:], -1.0, border_meta.dtype)

    pl.semaphore_wait(barrier, 4 * near + 3)
    own_copy = pltpu.make_async_copy(sendbuf.at[me], recv.at[2 * home + core], own_sem)
    own_copy.start()
    announce()
    meta_copies = [
        remote(meta_ref, border_meta.at[0], msend_sem.at[0], mrecv_sem.at[0], nxt_id),
        remote(meta_ref, border_meta.at[1], msend_sem.at[1], mrecv_sem.at[1], prv_id),
    ]
    pl.when(has_nxt)(meta_copies[0].start)
    pl.when(has_prv)(meta_copies[1].start)
    for kind, value in plan:
        if kind == "send":
            for place in range(*batches[value]):
                send(place)
        elif kind == "relay":
            relay(value)
        elif kind == "sent":
            sent(value)
        else:
            pl.semaphore_wait(ready_sem, 2)

    def rows_of(part):
        return part.astype(jnp.float32).reshape(8 * freqs, BS).astype(jnp.bfloat16)

    def place_band(row, block, offsets):
        for shift in range(3):
            parts = []
            for part in range(2):
                total = None
                for slot in range(SLOTS):
                    first = slot * PAIR + part * BS
                    live = jnp.where(offsets[slot] == float(shift), block[first : first + BS], 0.0)
                    total = live if total is None else total + live
                parts.append(total)
            bands[row, shift, :BS, :BS] = parts[0].astype(jnp.bfloat16)
            bands[row, shift, :BS, BS:] = parts[1].astype(jnp.bfloat16)
            bands[row, shift, BS:, :BS] = (-parts[1]).astype(jnp.bfloat16)
            bands[row, shift, BS:, BS:] = parts[0].astype(jnp.bfloat16)

    def assemble(rows, offsets, first):
        joined = jnp.concatenate([rows_of(row) for row in rows], axis=1)
        blocks = jnp.dot(gather[...], joined, preferred_element_type=jnp.float32)
        for n in range(len(rows)):
            place_band(first + n, blocks[:, n * BS : (n + 1) * BS], offsets[n])

    scale = (3.0 * BS) ** (-0.5)

    def band_term(row, source, inner):
        return jnp.dot(
            bands[row, source, :BS, :], bands[row + source - 1, inner],
            preferred_element_type=jnp.float32,
        )

    def first_term(row, source, inner):
        return jnp.dot(
            bands[row, source, :BS, :], firsts[row + source - 2, inner],
            preferred_element_type=jnp.float32,
        )

    def keep_first(row, target, total):
        value = (total * scale).astype(jnp.bfloat16)
        firsts[row - 1, target, :BS, :] = value
        firsts[row - 1, target, BS:, :BS] = -value[:, BS:]
        firsts[row - 1, target, BS:, BS:] = value[:, :BS]

    def total_of(term, row, target, sources):
        terms = [
            term(row, source, target - source + 1)
            for source in sources
            if 0 <= target - source + 1 <= 2
        ]
        return sum(terms[1:], terms[0]) if terms else jnp.zeros((BS, PAIR), jnp.float32)

    def finish(index):
        results = [
            firsts[index + 1, target, :BS, :].astype(jnp.float32) - seconds[index, target] * scale
            for target in range(3)
        ]
        for slot in range(SLOTS):
            offset = meta_ref[pl.ds(2 * index + slot, 1), :]
            for part in range(2):
                span = slice(part * BS, (part + 1) * BS)
                chosen = [
                    jnp.where(offset == float(target), results[target][:, span], 0.0)
                    for target in range(3)
                ]
                out_ref[0, part, index, slot] = (chosen[0] + chosen[1] + chosen[2]).astype(jnp.bfloat16)

    own_offsets = [
        [meta_ref[2 * n + slot : 2 * n + slot + 1, :] for slot in range(SLOTS)] for n in range(ROWS)
    ]
    assemble([recv[:, 0], recv[:, 1]], own_offsets[:2], 2)
    assemble([recv[:, 2]], own_offsets[2:], 4)
    for target in range(3):
        keep_first(3, target, total_of(band_term, 3, target, range(3)))
        partial[0, target] = total_of(band_term, 2, target, (1, 2))
        partial[1, target] = total_of(band_term, 4, target, (0, 1))
    for target in range(3):
        seconds[0, target] = total_of(first_term, 2, target, (2,))
        seconds[1, target] = total_of(first_term, 3, target, (1,))
        seconds[2, target] = total_of(first_term, 4, target, (0,))

    for side, there in ((1, has_nxt), (0, has_prv)):

        @pl.when(there)
        def _(side=side):
            mine, whole = border_meta.at[side], border.at[side]
            remote(mine, mine, msend_sem.at[side], mrecv_sem.at[side], prv_id).wait_recv()
            remote(whole, whole, fsend_sem.at[side], frecv_sem.at[side], prv_id).wait_recv()

        lines = [2 * n + 2 - 2 * side for n in range(2)]
        offsets = [
            [border_meta[side, line + slot : line + slot + 1, :] for slot in range(SLOTS)]
            for line in lines
        ]
        assemble([border[side, :, 0], border[side, :, 1]], offsets, 5 * side)
    for side in range(2):
        outer, inner = 1 + 4 * side, 2 + 2 * side
        for target in (1 - side, 2 - side):
            keep_first(outer, target, total_of(band_term, outer, target, range(3)))
        for target in range(3):
            keep_first(
                inner, target,
                partial[side, target] + total_of(band_term, inner, target, (2 * side,)),
            )
    for side in range(2):
        inner = 2 + 2 * side
        for target in range(3):
            seconds[2 * side, target] += total_of(first_term, inner, target, (2 * side, 1))
        finish(2 * side)
    for target in range(3):
        seconds[1, target] += total_of(first_term, 3, target, (0, 2))
    finish(1)

    for batch in range(len(batches)):
        if ("sent", batch) not in plan:
            sent(batch)
    for side, there in enumerate((has_nxt, has_prv)):

        @pl.when(there)
        def _(side=side):
            whole = border.at[side]
            remote(whole, whole, fsend_sem.at[side], frecv_sem.at[side], prv_id).wait_send()
            meta_copies[side].wait_send()


def schedule(chips):
    def both(*reaches):
        return [step for reach in reaches for step in (reach, -reach)]

    groups = [both(8,7), both(6)+[0], [16]+both(15,14), both(13,12,11), both(10,9), both(5,4), both(3,2,1)]
    order = [step for group in groups for step in group]
    cuts = [sum(len(group) for group in groups[:n]) for n in range(len(groups) + 1)]
    batches = list(zip(cuts[:-1], cuts[1:]))
    hops = (8, 8)
    plan = [('send', 0), ('send', 1), ('ready', 0), ('send', 2), ('send', 3), ('send', 4), ('relay', 0), ('relay', 1), ('relay', 2), ('send', 5), ('send', 6), ('relay', 3), ('relay', 4), ('relay', 5), ('relay', 6)]
    return order, batches, plan, hops


def solution(mesh):
    freqs, srows, rcols = mesh.shape["freq"], mesh.shape["srow"], mesh.shape["rcol"]

    def per_device(data_time, block_cols, row_counts):
        samples = data_time.shape[-1]
        pairs = ROWS * SLOTS
        chips = freqs // 2
        order, batches, plan, hops = schedule(chips)
        return pl.pallas_call(
            functools.partial(kernel, freqs, srows, rcols, order, batches, plan, hops),
            out_shape=jax.ShapeDtypeStruct((1, 2, ROWS, SLOTS, BS, BS), jnp.bfloat16),
            in_specs=[
                pl.BlockSpec(memory_space=pl.ANY),
                pl.BlockSpec(memory_space=pl.ANY),
                pl.BlockSpec(memory_space=pl.ANY),
            ],
            out_specs=pl.BlockSpec(memory_space=pltpu.VMEM),
            scratch_shapes=[
                pltpu.VMEM((pairs, PAIR, samples), jnp.bfloat16),
                pltpu.VMEM((2 * freqs, samples), jnp.bfloat16),
                pltpu.VMEM((SLOTS, ROWS), jnp.int32),
                pltpu.VMEM((1, ROWS), jnp.int32),
                pltpu.VMEM((8, BS), jnp.float32),
                pltpu.VMEM(((freqs + 1) * ROWS * 8, BS), jnp.float32),
                pltpu.VMEM((freqs, ROWS, 8, BS), jnp.bfloat16),
                pltpu.VMEM((freqs, ROWS, 8, BS), jnp.bfloat16),
                pltpu.VMEM((2, freqs, 2, 8, BS), jnp.bfloat16),
                pltpu.VMEM((2, 8, BS), jnp.float32),
                pltpu.VMEM((8 * freqs, 8 * freqs), jnp.bfloat16),
                pltpu.VMEM((7, 3, PAIR, PAIR), jnp.bfloat16),
                pltpu.VMEM((5, 3, PAIR, PAIR), jnp.bfloat16),
                pltpu.VMEM((2, 3, BS, PAIR), jnp.float32),
                pltpu.VMEM((ROWS, 3, BS, PAIR), jnp.float32),
                pltpu.SemaphoreType.DMA((pairs,)),
                pltpu.SemaphoreType.DMA((2,)),
                pltpu.SemaphoreType.DMA,
                pltpu.SemaphoreType.REGULAR,
                pltpu.SemaphoreType.DMA((len(batches),)),
                pltpu.SemaphoreType.DMA((len(batches),)),
                pltpu.SemaphoreType.DMA((2,)),
                pltpu.SemaphoreType.DMA((2,)),
                pltpu.SemaphoreType.DMA((2,)),
                pltpu.SemaphoreType.DMA((2,)),
            ],
            compiler_params=pltpu.CompilerParams(
                collective_id=0, has_side_effects=True, vmem_limit_bytes=40 * 1024 * 1024
            ),
        )(
            *(
                pltpu.with_memory_space_constraint(value, pltpu.HBM)
                for value in (
                    data_time.reshape(pairs, PAIR, samples),
                    block_cols.T,
                    row_counts.reshape(1, ROWS),
                )
            )
        )

    return jax.shard_map(
        per_device,
        mesh=mesh,
        in_specs=(
            P(("srow", "rcol"), None, "freq", None, None),
            P(("srow", "rcol"), None),
            P(("srow", "rcol")),
        ),
        out_specs=P("freq", None, ("srow", "rcol"), None, None, None),
        check_vma=False,
    )
```

```python
import functools
import math

import jax
import jax.numpy as jnp
from jax import lax
from jax.experimental import pallas as pl
from jax.experimental.pallas import tpu as pltpu
from jax.sharding import PartitionSpec as P

BS = 128
PAIR = 2 * BS
ROWS = 3
SLOTS = 2
MESH = pl.DeviceIdType.MESH


def spectral_table(samples, freqs):
    row = lax.broadcasted_iota(jnp.int32, (2 * freqs, samples), 0)
    time = lax.broadcasted_iota(jnp.int32, (2 * freqs, samples), 1)
    part = (row >= freqs).astype(jnp.int32)
    phase = ((row - part * freqs + 1) * time + part * (samples // 4)) & (samples - 1)
    folded = jnp.abs(phase - samples // 2) - samples // 4
    angle = folded.astype(jnp.float32) * (2.0 * math.pi / samples)
    square = angle * angle
    value = jnp.full_like(square, -1.0 / math.factorial(11))
    for power in (9, 7, 5, 3, 1):
        value = value * square + (-1.0) ** (power // 2) / math.factorial(power)
    return (value * angle * (1.0 / math.sqrt(samples))).astype(jnp.bfloat16)


def kernel(
    freqs, srows, rcols, order, batches, plan, hops,
    x_hbm, cols_hbm, counts_hbm, out_ref,
    xv, tv, cols_ref, counts_ref, meta_ref, spread, sendbuf, recv, border, border_meta, gather, bands, firsts, partial, seconds,
    load_sem, index_sem, own_sem, ready_sem, send_sem, recv_sem, fsend_sem, frecv_sem, msend_sem, mrecv_sem,
):
    chips = freqs // 2
    me = lax.axis_index("freq")
    zpos, core = me // 2, me % 2
    grow = lax.axis_index("srow") * rcols + lax.axis_index("rcol")
    groups = srows * rcols
    nxt, prv = (grow + 1) % groups, (grow + groups - 1) % groups
    has_nxt, has_prv = grow < groups - 1, grow > 0
    nxt_id = (me, nxt // rcols, nxt % rcols)
    prv_id = (me, prv // rcols, prv % rcols)
    pairs = ROWS * SLOTS
    home = order.index(0)

    loads = [pltpu.make_async_copy(x_hbm.at[n], xv.at[n], load_sem.at[n]) for n in range(pairs)]
    index_copies = [
        pltpu.make_async_copy(cols_hbm, cols_ref, index_sem.at[0]),
        pltpu.make_async_copy(counts_hbm, counts_ref, index_sem.at[1]),
    ]
    for load in loads + index_copies:
        load.start()

    near, further = hops
    barrier = pltpu.get_barrier_semaphore()
    for reach in range(near, -1, -1):
        for way in (1, -1):
            chip = (zpos + chips + way * reach) % chips
            for other in range(2):
                if reach or (way, other) == (1, 0):
                    pl.semaphore_signal(
                        barrier,
                        inc=1,
                        device_id={"freq": 2 * chip + (other if reach else 1 - core)},
                        device_id_type=MESH,
                    )
    pl.semaphore_signal(barrier, inc=1, device_id=nxt_id, device_id_type=MESH)
    pl.semaphore_signal(barrier, inc=1, device_id=prv_id, device_id_type=MESH)

    tv[...] = spectral_table(tv.shape[1], freqs)
    for n in range(pairs):
        loads[n].wait()
        row, slot = n // SLOTS, n % SLOTS
        value = lax.dot_general(
            tv[...], xv[n], (((1,), (1,)), ((), ())), preferred_element_type=jnp.float32
        )
        for part in range(2):
            for trace in range(2):
                place = row * 8 + part * 4 + slot * 2 + trace
                spread[pl.ds(place, freqs, stride=ROWS * 8), :] = value[
                    part * freqs : (part + 1) * freqs, trace * BS : (trace + 1) * BS
                ]
    sendbuf[...] = spread[: freqs * ROWS * 8, :].reshape(freqs, ROWS, 8, BS).astype(jnp.bfloat16)

    def remote(src, dst, ssem, rsem, target):
        return pltpu.make_async_remote_copy(
            src_ref=src, dst_ref=dst, send_sem=ssem, recv_sem=rsem,
            device_id=target, device_id_type=MESH,
        )

    def send(place):
        chip = (zpos + chips + (1 - 2 * core) * order[place]) % chips
        batch = [low <= place < high for low, high in batches].index(True)
        for other in range(2):
            target = 2 * chip + (other if order[place] else 1 - core)
            if order[place] or other == 0:
                remote(
                    sendbuf.at[target], recv.at[2 * place + core], send_sem.at[batch], recv_sem.at[batch],
                    {"freq": target},
                ).start()

    def sent(batch):
        low, high = batches[batch]
        span = recv.at[pl.ds(2 * low, 2 * (high - low) - (low <= home < high))]
        remote(span, span, send_sem.at[batch], recv_sem.at[batch], prv_id).wait_send()

    def relay(batch):
        low, high = batches[batch]
        mine = low <= home < high
        low, high = 2 * low, 2 * high
        arrived = recv.at[pl.ds(low, high - low - mine)]
        remote(arrived, arrived, send_sem.at[batch], recv_sem.at[batch], prv_id).wait_recv()
        if mine:
            own_copy.wait()
        span = pl.ds(low, high - low)
        down = remote(
            recv.at[span, pl.ds(0, 2)], border.at[1, span], fsend_sem.at[1], frecv_sem.at[1], prv_id
        )
        up = remote(
            recv.at[span, pl.ds(1, 2)], border.at[0, span], fsend_sem.at[0], frecv_sem.at[0], nxt_id
        )
        pl.when(has_nxt)(up.start)
        pl.when(has_prv)(down.start)

    def announce():
        for way in (1, chips - 1):
            pl.semaphore_signal(
                ready_sem,
                inc=1,
                device_id={"freq": 2 * ((zpos + way * further) % chips) + core},
                device_id_type=MESH,
            )

    pl.semaphore_wait(barrier, 4 * near + 3)
    own_copy = pltpu.make_async_copy(sendbuf.at[me], recv.at[2 * home + core], own_sem)
    own_copy.start()
    announce()
    def follow(steps):
        for kind, value in steps:
            if kind == "send":
                for place in range(*batches[value]):
                    send(place)
            elif kind == "relay":
                relay(value)
            elif kind == "sent":
                sent(value)
            else:
                pl.semaphore_wait(ready_sem, 2)

    cut = [kind for kind, _ in plan].index("ready")
    follow(plan[:cut])

    for copy in index_copies:
        copy.wait()
    for row in range(ROWS):
        for slot in range(SLOTS):
            offset = cols_ref[slot : slot + 1, row : row + 1] - (ROWS * grow + row) + 1
            offset = jnp.where(counts_ref[:, row : row + 1] > slot, offset, -1)
            meta_ref[2 * row + slot : 2 * row + slot + 1, :] = jnp.broadcast_to(
                offset.astype(jnp.float32), (1, BS)
            )
    meta_ref[pairs:, :] = jnp.full((8 - pairs, BS), -1.0, jnp.float32)

    for side, there in enumerate((has_prv, has_nxt)):

        @pl.when(jnp.logical_not(there))
        def _(side=side):
            border[side] = jnp.zeros(border.shape[1:], border.dtype)
            border_meta[side] = jnp.full(border_meta.shape[1:], -1.0, border_meta.dtype)

    meta_copies = [
        remote(meta_ref, border_meta.at[0], msend_sem.at[0], mrecv_sem.at[0], nxt_id),
        remote(meta_ref, border_meta.at[1], msend_sem.at[1], mrecv_sem.at[1], prv_id),
    ]
    pl.when(has_nxt)(meta_copies[0].start)
    pl.when(has_prv)(meta_copies[1].start)

    arrival = lax.broadcasted_iota(jnp.int32, (1, 8 * freqs), 1)
    came = jnp.zeros_like(arrival)
    for place, chip in enumerate(order):
        came = jnp.where(arrival >> 4 == place, chip, came)
    from_core = (arrival >> 3) & 1
    origin = ((zpos + chips - (1 - 2 * from_core) * came) & (chips - 1)) * 2 + from_core
    key_in = origin * 8 + (arrival & 7)
    place = lax.broadcasted_iota(jnp.int32, (8 * freqs, 1), 0)
    trace_index = place & (BS - 1)
    key_out = (
        (trace_index >> 1) * 8
        + ((place >> 7) & 1) * 4
        + ((place >> 8) & 1) * 2
        + (trace_index & 1)
    )
    gather[...] = jnp.where(key_in == key_out, 1.0, 0.0).astype(jnp.bfloat16)

    follow(plan[cut:])

    def rows_of(part):
        return part.astype(jnp.float32).reshape(8 * freqs, BS).astype(jnp.bfloat16)

    def place_band(row, block, offsets):
        for shift in range(3):
            parts = []
            for part in range(2):
                total = None
                for slot in range(SLOTS):
                    first = slot * PAIR + part * BS
                    live = jnp.where(offsets[slot] == float(shift), block[first : first + BS], 0.0)
                    total = live if total is None else total + live
                parts.append(total)
            bands[row, shift, :BS, :BS] = parts[0].astype(jnp.bfloat16)
            bands[row, shift, :BS, BS:] = parts[1].astype(jnp.bfloat16)
            bands[row, shift, BS:, :BS] = (-parts[1]).astype(jnp.bfloat16)
            bands[row, shift, BS:, BS:] = parts[0].astype(jnp.bfloat16)

    def assemble(rows, offsets, first):
        joined = jnp.concatenate([rows_of(row) for row in rows], axis=1)
        blocks = jnp.dot(gather[...], joined, preferred_element_type=jnp.float32)
        for n in range(len(rows)):
            place_band(first + n, blocks[:, n * BS : (n + 1) * BS], offsets[n])

    scale = (3.0 * BS) ** (-0.5)

    def band_term(row, source, inner):
        return jnp.dot(
            bands[row, source, :BS, :], bands[row + source - 1, inner],
            preferred_element_type=jnp.float32,
        )

    def first_term(row, source, inner):
        return jnp.dot(
            bands[row, source, :BS, :], firsts[row + source - 2, inner],
            preferred_element_type=jnp.float32,
        )

    def keep_first(row, target, total):
        value = (total * scale).astype(jnp.bfloat16)
        firsts[row - 1, target, :BS, :] = value
        firsts[row - 1, target, BS:, :BS] = -value[:, BS:]
        firsts[row - 1, target, BS:, BS:] = value[:, :BS]

    def total_of(term, row, target, sources):
        terms = [
            term(row, source, target - source + 1)
            for source in sources
            if 0 <= target - source + 1 <= 2
        ]
        return sum(terms[1:], terms[0]) if terms else jnp.zeros((BS, PAIR), jnp.float32)

    def finish(index):
        results = [
            firsts[index + 1, target, :BS, :].astype(jnp.float32) - seconds[index, target] * scale
            for target in range(3)
        ]
        for slot in range(SLOTS):
            offset = meta_ref[pl.ds(2 * index + slot, 1), :]
            for part in range(2):
                span = slice(part * BS, (part + 1) * BS)
                chosen = [
                    jnp.where(offset == float(target), results[target][:, span], 0.0)
                    for target in range(3)
                ]
                out_ref[0, part, index, slot] = (chosen[0] + chosen[1] + chosen[2]).astype(jnp.bfloat16)

    own_offsets = [
        [meta_ref[2 * n + slot : 2 * n + slot + 1, :] for slot in range(SLOTS)] for n in range(ROWS)
    ]
    assemble([recv[:, 0], recv[:, 1]], own_offsets[:2], 2)
    assemble([recv[:, 2]], own_offsets[2:], 4)
    for target in range(3):
        keep_first(3, target, total_of(band_term, 3, target, range(3)))
        partial[0, target] = total_of(band_term, 2, target, (1, 2))
        partial[1, target] = total_of(band_term, 4, target, (0, 1))
    for target in range(3):
        seconds[0, target] = total_of(first_term, 2, target, (2,))
        seconds[1, target] = total_of(first_term, 3, target, (1,))
        seconds[2, target] = total_of(first_term, 4, target, (0,))

    for side, there in ((1, has_nxt), (0, has_prv)):

        @pl.when(there)
        def _(side=side):
            mine, whole = border_meta.at[side], border.at[side]
            remote(mine, mine, msend_sem.at[side], mrecv_sem.at[side], prv_id).wait_recv()
            remote(whole, whole, fsend_sem.at[side], frecv_sem.at[side], prv_id).wait_recv()

        lines = [2 * n + 2 - 2 * side for n in range(2)]
        offsets = [
            [border_meta[side, line + slot : line + slot + 1, :] for slot in range(SLOTS)]
            for line in lines
        ]
        assemble([border[side, :, 0], border[side, :, 1]], offsets, 5 * side)
    for side in range(2):
        outer, inner = 1 + 4 * side, 2 + 2 * side
        for target in (1 - side, 2 - side):
            keep_first(outer, target, total_of(band_term, outer, target, range(3)))
        for target in range(3):
            keep_first(
                inner, target,
                partial[side, target] + total_of(band_term, inner, target, (2 * side,)),
            )
    for side in range(2):
        inner = 2 + 2 * side
        for target in range(3):
            seconds[2 * side, target] += total_of(first_term, inner, target, (2 * side, 1))
        finish(2 * side)
    for target in range(3):
        seconds[1, target] += total_of(first_term, 3, target, (0, 2))
    finish(1)

    for batch in range(len(batches)):
        if ("sent", batch) not in plan:
            sent(batch)
    for side, there in enumerate((has_nxt, has_prv)):

        @pl.when(there)
        def _(side=side):
            whole = border.at[side]
            remote(whole, whole, fsend_sem.at[side], frecv_sem.at[side], prv_id).wait_send()
            meta_copies[side].wait_send()


def schedule(chips):
    def both(*reaches):
        return [step for reach in reaches for step in (reach, -reach)]

    groups = [both(8,7), both(6)+[0], [16]+both(15,14), both(13,12,11), both(10,9), both(5,4), both(3,2,1)]
    order = [step for group in groups for step in group]
    cuts = [sum(len(group) for group in groups[:n]) for n in range(len(groups) + 1)]
    batches = list(zip(cuts[:-1], cuts[1:]))
    hops = (8, 8)
    plan = [('send', 0), ('send', 1), ('ready', 0), ('send', 2), ('send', 3), ('send', 4), ('relay', 0), ('relay', 1), ('relay', 2), ('send', 5), ('send', 6), ('relay', 3), ('relay', 4), ('relay', 5), ('relay', 6)]
    return order, batches, plan, hops


def solution(mesh):
    freqs, srows, rcols = mesh.shape["freq"], mesh.shape["srow"], mesh.shape["rcol"]

    def per_device(data_time, block_cols, row_counts):
        samples = data_time.shape[-1]
        pairs = ROWS * SLOTS
        chips = freqs // 2
        order, batches, plan, hops = schedule(chips)
        return pl.pallas_call(
            functools.partial(kernel, freqs, srows, rcols, order, batches, plan, hops),
            out_shape=jax.ShapeDtypeStruct((1, 2, ROWS, SLOTS, BS, BS), jnp.bfloat16),
            in_specs=[
                pl.BlockSpec(memory_space=pl.ANY),
                pl.BlockSpec(memory_space=pl.ANY),
                pl.BlockSpec(memory_space=pl.ANY),
            ],
            out_specs=pl.BlockSpec(memory_space=pltpu.VMEM),
            scratch_shapes=[
                pltpu.VMEM((pairs, PAIR, samples), jnp.bfloat16),
                pltpu.VMEM((2 * freqs, samples), jnp.bfloat16),
                pltpu.VMEM((SLOTS, ROWS), jnp.int32),
                pltpu.VMEM((1, ROWS), jnp.int32),
                pltpu.VMEM((8, BS), jnp.float32),
                pltpu.VMEM(((freqs + 1) * ROWS * 8, BS), jnp.float32),
                pltpu.VMEM((freqs, ROWS, 8, BS), jnp.bfloat16),
                pltpu.VMEM((freqs, ROWS, 8, BS), jnp.bfloat16),
                pltpu.VMEM((2, freqs, 2, 8, BS), jnp.bfloat16),
                pltpu.VMEM((2, 8, BS), jnp.float32),
                pltpu.VMEM((8 * freqs, 8 * freqs), jnp.bfloat16),
                pltpu.VMEM((7, 3, PAIR, PAIR), jnp.bfloat16),
                pltpu.VMEM((5, 3, PAIR, PAIR), jnp.bfloat16),
                pltpu.VMEM((2, 3, BS, PAIR), jnp.float32),
                pltpu.VMEM((ROWS, 3, BS, PAIR), jnp.float32),
                pltpu.SemaphoreType.DMA((pairs,)),
                pltpu.SemaphoreType.DMA((2,)),
                pltpu.SemaphoreType.DMA,
                pltpu.SemaphoreType.REGULAR,
                pltpu.SemaphoreType.DMA((len(batches),)),
                pltpu.SemaphoreType.DMA((len(batches),)),
                pltpu.SemaphoreType.DMA((2,)),
                pltpu.SemaphoreType.DMA((2,)),
                pltpu.SemaphoreType.DMA((2,)),
                pltpu.SemaphoreType.DMA((2,)),
            ],
            compiler_params=pltpu.CompilerParams(
                collective_id=0, has_side_effects=True, vmem_limit_bytes=40 * 1024 * 1024
            ),
        )(
            *(
                pltpu.with_memory_space_constraint(value, pltpu.HBM)
                for value in (
                    data_time.reshape(pairs, PAIR, samples),
                    block_cols.T,
                    row_counts.reshape(1, ROWS),
                )
            )
        )

    return jax.shard_map(
        per_device,
        mesh=mesh,
        in_specs=(
            P(("srow", "rcol"), None, "freq", None, None),
            P(("srow", "rcol"), None),
            P(("srow", "rcol")),
        ),
        out_specs=P("freq", None, ("srow", "rcol"), None, None, None),
        check_vma=False,
    )
```
